32 devices in a mesh: seq: 4 (over y, x), chan: 8 (over z, core).
Axes of the slice: x: 2, y: 2, z: 4, core: 2. Of those that a mesh axis runs over, the one named last changes fastest.
Arguments:
- inputs: bfloat16 [4096, 1024], P('chan', 'seq'), may hold values from -0.1875 to 0.1875
- grad_out: bfloat16 [4096, 1024], P('chan', 'seq'), may hold values from -6 to 6
- filt: bfloat16 [4096, 1024], P('chan', 'seq'), may hold values from -0.1875 to 0.1875
- rates: float32 [4096], P('chan'), may hold values from 0.5 to 50
- mix_weight: bfloat16 [4096, 64], P('chan'), may hold values from -0.09375 to 0.09375
Outputs:
- grad_in: bfloat16 [4096, 1024], P('chan', 'seq')
- grad_filt: float32 [4096, 1024], P('chan', 'seq')
- grad_hidden: float32 [64, 1024], P(None, 'seq')
The draws below stay inside these ranges and needn't reach their ends.
All inputs are finite; a program needn't handle non-finite values.
Results may differ from the reference program's by a relative error of at most 0.0085.
Values may be sent and summed in bfloat16 or wider, within the bound.
No kernel may reach another device: no remote copies, remote signals or barrier semaphores. Data moves between devices by JAX's collectives and lax.ppermute only.
A program may use at most 64 MiB of HBM per device.

```python
import math
import jax
import jax.numpy as jnp
from jax import lax

D = 4096
K = 64
S = 1024


def block_levels(key, shape, shards, low, largest):
    def one(position, shards_of):
        draws = jax.random.uniform(jax.random.fold_in(jax.random.fold_in(key, 6), position), (shards_of,), jnp.float32, low / len(shards), largest / len(shards))
        return jnp.repeat(jnp.exp(draws), shape[position] // shards_of).reshape((-1,) + (1,) * (len(shape) - position - 1))

    loudness = one(*shards[0])
    for cut in shards[1:]:
        loudness = loudness * one(*cut)
    return loudness


def normal_values(own_key, extent, spread, reach, split=(), kind=jnp.bfloat16):
    gain = block_levels(own_key, extent, split, -0.22, 0.18) if split else 1.0
    drawn = jax.random.normal(own_key, extent, jnp.float32) * spread * gain
    return jnp.minimum(jnp.maximum(drawn, -reach), reach).astype(kind)


def setup_inputs(seed: int = 0) -> dict:
    seeds = jax.random.split(jax.random.key(seed), 6)
    return {
        "inputs": normal_values(seeds[0], (D, S), S ** -0.5, 0.1875, ((0, 8), (1, 4))),
        "grad_out": normal_values(seeds[1], (D, S), 1.0, 6.0, ((0, 8), (1, 4))),
        "filt": normal_values(seeds[2], (D, S), S ** -0.5, 0.1875, ((0, 8), (1, 4))),
        "rates": jnp.clip(jnp.exp(math.log(50.0) - 4.6051702 * jax.random.uniform(seeds[3], (D,), jnp.float32) ** block_levels(seeds[3], (D,), ((0, 8),), -0.2, 0.2)), 0.5, 50.0),
        "mix_weight": normal_values(seeds[4], (D, K), D ** -0.5, 0.09375, ((0, 8),)),
    }


def reference(inputs, grad_out, filt, rates, mix_weight):
    length = S
    period = 2 * S
    values_in = inputs.astype(jnp.float32)
    values_dy = grad_out.astype(jnp.float32)
    values_h = filt.astype(jnp.float32)
    conv_back = jnp.fft.irfft(jnp.fft.rfft(values_h, period, axis=1) * jnp.fft.rfft(values_dy[:, ::-1], period, axis=1), period, axis=1)
    grad_in = conv_back[:, :length][:, ::-1]
    conv_lag = jnp.fft.irfft(jnp.fft.rfft(values_dy, period, axis=1) * jnp.fft.rfft(values_in[:, ::-1], period, axis=1), period, axis=1)
    grad_filt = conv_lag[:, length - 1:2 * length - 1]
    lags = jnp.arange(length, dtype=jnp.int32).astype(jnp.float32)
    decay = jnp.exp(-rates[:, None] * lags[None, :] / S)
    grad_hidden = jnp.dot(mix_weight.astype(jnp.float32).T, grad_filt * decay, precision=lax.Precision.HIGHEST, preferred_element_type=jnp.float32)
    return grad_in.astype(jnp.bfloat16), grad_filt.astype(jnp.float32), grad_hidden
```

```python
import functools

import jax
import jax.numpy as jnp
import ml_dtypes
import numpy as np
from jax import lax
from jax.experimental import pallas as pl
from jax.experimental.pallas import tpu as pltpu
from jax.sharding import PartitionSpec as P

F32 = jnp.float32
BF16 = jnp.bfloat16


def tables(block):
    k = np.concatenate([np.arange(0, block, 2), np.arange(1, block, 2)]).astype(np.float64)
    phase = np.pi * (k[None, :] + 0.5) * np.arange(block, dtype=np.float64)[:, None] / block
    forward = np.concatenate([np.cos(phase), -np.sin(phase)], axis=1)
    back = forward.T / block
    return forward.astype(ml_dtypes.bfloat16), back.astype(ml_dtypes.bfloat16)


def dot(left, right):
    return jnp.dot(left, right, preferred_element_type=F32)


def xor_permute(value, axis, size, k):
    return lax.ppermute(value, axis, [(j, j ^ k) for j in range(size)])


def correlate(rows, block, spec_g, spec_z, prod):
    half = block // 2
    step = 16

    def chunk(c, carry):
        at = pl.ds(pl.multiple_of(c * step, step), step)
        for part, sign in ((0, 1.0), (1, -1.0)):
            re = pl.ds(part * half, half)
            im = pl.ds(block + part * half, half)
            g = [(spec_g[j, at, re], spec_g[j, at, im]) for j in range(4)]
            z = [(spec_z[j, at, re], spec_z[j, at, im]) for j in range(4)]
            later = None
            for d in (3, 2, 1, 0):
                sum_re = sum_im = None
                for j in range(d, 4):
                    gr, gi = g[j]
                    zr, zi = z[j - d]
                    term_re = gr * zr + gi * zi
                    term_im = gi * zr - gr * zi
                    sum_re = term_re if sum_re is None else sum_re + term_re
                    sum_im = term_im if sum_im is None else sum_im + term_im
                if later is None:
                    out_re, out_im = sum_re, sum_im
                elif sign > 0:
                    out_re, out_im = sum_re + later[1], sum_im - later[0]
                else:
                    out_re, out_im = sum_re - later[1], sum_im + later[0]
                prod[d, at, re] = out_re.astype(BF16)
                prod[d, at, im] = out_im.astype(BF16)
                later = (sum_re, sum_im)
        return carry

    lax.fori_loop(0, rows // step, chunk, 0)


def filter_kernel(rows, block, total, s0, s1, s2, s3, table, back, rates_ref, mix_ref, *refs):
    filt_out, hidden_out, (spec_g, spec_z, prod) = refs[:4], refs[4:8], refs[8:]
    me = lax.axis_index("seq")
    for k, slot in enumerate((s0, s1, s2, s3)):
        spec = dot(slot[...], table[...])
        spec_g[me ^ k] = spec[:rows]
        spec_z[me ^ k] = spec[rows:]
    correlate(rows, block, spec_g, spec_z, prod)
    mine = pl.ds(pl.multiple_of(me * rows, rows), rows)
    rates = jnp.broadcast_to(rates_ref[:, mine], (block, rows)).T
    mix = mix_ref[:, mine]
    for k in range(4):
        values = dot(prod[me ^ k], back[...])
        lags = lax.broadcasted_iota(jnp.int32, (rows, block), 1) + (me ^ k) * block
        windowed = values * jnp.exp(-rates * lags.astype(F32) / total)
        high = windowed.astype(BF16)
        low = (windowed - high.astype(F32)).astype(BF16)
        hidden = dot(mix, high) + dot(mix, low)
        filt_out[k][...] = values.astype(filt_out[k].dtype)
        hidden_out[k][...] = hidden.astype(hidden_out[k].dtype)


def input_kernel(rows, block, s0, s1, s2, s3, f0, f1, f2, f3, w1, w2, w3, table, back, *refs):
    outs, (spec_g, spec_z, prod) = refs[:4], refs[4:]
    me = lax.axis_index("seq")
    for k, (slot, f) in enumerate(((s0, f0), (s1, f1), (s2, f2), (s3, f3))):
        spec_g[me ^ k] = dot(slot[:rows], table[...])
        spec_z[me ^ k] = dot(f[...], table[...])
    correlate(rows, block, spec_g, spec_z, prod)
    for k, out in enumerate(outs):
        out[:rows] = dot(prod[me ^ k], back[...]).astype(BF16)
    for out, w in zip(outs[1:], (w1, w2, w3)):
        out[rows:] = w[...]


def sum_kernel(h0, h1, h2, h3, after, out, sent):
    del after
    total = (h0[...] + h1[...].astype(F32)) + (h2[...].astype(F32) + h3[...].astype(F32))
    out[...] = total
    sent[...] = total.astype(BF16)


def unpack_kernel(rows, w0, v0, r1, r2, r3, filt_out, in_out):
    me = lax.axis_index("seq")
    filt_out[me] = w0[...]
    in_out[me] = v0[...]
    for k, r in enumerate((r1, r2, r3), 1):
        in_out[me ^ k] = r[:rows]
        filt_out[me ^ k] = r[rows:].astype(F32)


def body_four(channel_axis, inputs, grad_out, filt, rates, mix_weight):
    channels, block = inputs.shape
    rows = channels // 4
    total = 4 * block
    hidden = mix_weight.shape[1]
    forward, back = (jnp.asarray(t) for t in tables(block))
    shape = jax.ShapeDtypeStruct
    vmem = pl.BlockSpec(memory_space=pltpu.VMEM)
    params = pltpu.CompilerParams(vmem_limit_bytes=8 * 1024 * 1024)
    small = pltpu.CompilerParams(vmem_limit_bytes=2 * 1024 * 1024)
    cost = pl.CostEstimate(flops=1000, bytes_accessed=1000, transcendentals=0)
    scratch = [
        pltpu.VMEM((4, rows, 2 * block), F32),
        pltpu.VMEM((4, rows, 2 * block), F32),
        pltpu.VMEM((4, rows, 2 * block), BF16),
    ]

    me = lax.axis_index("seq")
    arrays = jnp.stack([value.reshape(4, rows, block) for value in (grad_out, inputs, filt)], 1)
    parts = [lax.dynamic_index_in_dim(arrays, me ^ k, 0, keepdims=False) for k in range(4)]
    slots = [p[:2].reshape(2 * rows, block) for p in parts]
    slots_f = [p[2] for p in parts]
    slots = slots[:1] + [xor_permute(slots[k], "seq", 4, k) for k in (1, 2, 3)]
    slots_f = slots_f[:1] + [xor_permute(slots_f[k], "seq", 4, k) for k in (1, 2, 3)]

    made = pl.pallas_call(
        functools.partial(filter_kernel, rows, block, total),
        out_shape=[shape((rows, block), F32)]
        + [shape((rows, block), BF16)] * 3
        + [shape((hidden, block), F32)]
        + [shape((hidden, block), BF16)] * 3,
        in_specs=[vmem] * 8,
        out_specs=[vmem] * 8,
        scratch_shapes=scratch,
        compiler_params=params,
        cost_estimate=cost,
    )(*slots, forward, back, rates.reshape(1, channels), mix_weight.T)

    got_hidden = [xor_permute(made[4 + k], "seq", 4, k) for k in (1, 2, 3)]

    made_in = pl.pallas_call(
        functools.partial(input_kernel, rows, block),
        out_shape=[shape((rows, block), BF16)] + [shape((2 * rows, block), BF16)] * 3,
        in_specs=[vmem] * 13,
        out_specs=[vmem] * 4,
        scratch_shapes=scratch,
        compiler_params=params,
        cost_estimate=cost,
    )(*slots, *slots_f, *made[1:4], forward, back)
    got = [xor_permute(made_in[k], "seq", 4, k) for k in (1, 2, 3)]

    partial, partial_sent = pl.pallas_call(
        sum_kernel,
        out_shape=[shape((hidden, block), F32), shape((hidden, block), BF16)],
        in_specs=[vmem] * 4 + [pl.BlockSpec(memory_space=pl.ANY)],
        out_specs=[vmem] * 2,
        compiler_params=small,
        cost_estimate=cost,
    )(made[4], *got_hidden, made_in[1])
    pair = partial + xor_permute(partial_sent, "chan", channel_axis, 1).astype(F32)
    pair_sent = pair.astype(BF16)
    grad_hidden = pair
    for k in range(2, channel_axis, 2):
        grad_hidden = grad_hidden + xor_permute(pair_sent, "chan", channel_axis, k).astype(F32)

    grad_filt, grad_in = pl.pallas_call(
        functools.partial(unpack_kernel, rows),
        out_shape=[shape((4, rows, block), F32), shape((4, rows, block), BF16)],
        in_specs=[vmem] * 5,
        out_specs=[vmem] * 2,
        compiler_params=small,
        cost_estimate=cost,
    )(made[0], made_in[0], *got)
    return grad_in.reshape(channels, block), grad_filt.reshape(channels, block), grad_hidden


def body_any(blocks, inputs, grad_out, filt, rates, mix_weight):
    channels, block = inputs.shape
    rows = channels // blocks
    total = blocks * block
    half = block // 2
    me = lax.axis_index("seq")
    forward, back = (jnp.asarray(t) for t in tables(block))
    sign = jnp.where(jnp.arange(block) < half, 1.0, -1.0).astype(F32)

    def spread(value):
        return lax.all_to_all(value.reshape(blocks, rows, block), "seq", 0, 0, tiled=True)

    def spectrum(value):
        spec = dot(value, forward)
        return spec[..., :block], spec[..., block:]

    def correlate_blocks(g, z):
        sums = []
        for d in range(blocks):
            gr, gi, zr, zi = g[0][d:], g[1][d:], z[0][: blocks - d], z[1][: blocks - d]
            sums.append(((gr * zr + gi * zi).sum(0), (gi * zr - gr * zi).sum(0)))
        sums.append((jnp.zeros_like(sums[0][0]),) * 2)
        out = [
            jnp.concatenate([sums[d][0] + sign * sums[d + 1][1], sums[d][1] - sign * sums[d + 1][0]], axis=-1)
            for d in range(blocks)
        ]
        return dot(jnp.stack(out).astype(BF16), back)

    spec_g = spectrum(spread(grad_out))
    grad_filt = correlate_blocks(spec_g, spectrum(spread(inputs)))
    grad_in = correlate_blocks(spec_g, spectrum(spread(filt)))
    grad_in = spread(grad_in.astype(BF16)).reshape(channels, block)
    grad_filt = lax.all_to_all(grad_filt, "seq", 0, 0, tiled=True).reshape(channels, block)
    lags = (me * block + jnp.arange(block, dtype=jnp.int32)).astype(F32)
    windowed = grad_filt * jnp.exp(-rates[:, None] * lags[None, :] / total)
    high = windowed.astype(BF16)
    low = (windowed - high.astype(F32)).astype(BF16)
    grad_hidden = lax.psum(dot(mix_weight.T, high) + dot(mix_weight.T, low), "chan")
    return grad_in, grad_filt, grad_hidden


def solution(mesh):
    blocks, chan = mesh.shape["seq"], mesh.shape["chan"]

    def body(inputs, grad_out, filt, rates, mix_weight):
        if blocks == 4 and chan & (chan - 1) == 0 and inputs.shape[0] % 512 == 0 and inputs.shape[1] % 256 == 0:
            return body_four(chan, inputs, grad_out, filt, rates, mix_weight)
        return body_any(blocks, inputs, grad_out, filt, rates, mix_weight)

    return jax.shard_map(
        body,
        mesh=mesh,
        in_specs=(P("chan", "seq"), P("chan", "seq"), P("chan", "seq"), P("chan"), P("chan", None)),
        out_specs=(P("chan", "seq"), P("chan", "seq"), P(None, "seq")),
        check_vma=False,
    )
```

```python
import functools

import jax
import jax.numpy as jnp
import ml_dtypes
import numpy as np
from jax import lax
from jax.experimental import pallas as pl
from jax.experimental.pallas import tpu as pltpu
from jax.sharding import PartitionSpec as P

F32 = jnp.float32
BF16 = jnp.bfloat16


def tables(block):
    k = np.concatenate([np.arange(0, block, 2), np.arange(1, block, 2)]).astype(np.float64)
    phase = np.pi * (k[None, :] + 0.5) * np.arange(block, dtype=np.float64)[:, None] / block
    forward = np.concatenate([np.cos(phase), -np.sin(phase)], axis=1)
    back = forward.T / block
    return forward.astype(ml_dtypes.bfloat16), back.astype(ml_dtypes.bfloat16)


def dot(left, right):
    return jnp.dot(left, right, preferred_element_type=F32)


def xor_permute(value, axis, size, k):
    return lax.ppermute(value, axis, [(j, j ^ k) for j in range(size)])


def correlate(rows, block, spec_g, spec_z, prod):
    half = block // 2
    step = 16

    def chunk(c, carry):
        at = pl.ds(pl.multiple_of(c * step, step), step)
        for part, sign in ((0, 1.0), (1, -1.0)):
            re = pl.ds(part * half, half)
            im = pl.ds(block + part * half, half)
            g = [(spec_g[j, at, re], spec_g[j, at, im]) for j in range(4)]
            z = [(spec_z[j, at, re], spec_z[j, at, im]) for j in range(4)]
            later = None
            for d in (3, 2, 1, 0):
                sum_re = sum_im = None
                for j in range(d, 4):
                    gr, gi = g[j]
                    zr, zi = z[j - d]
                    term_re = gr * zr + gi * zi
                    term_im = gi * zr - gr * zi
                    sum_re = term_re if sum_re is None else sum_re + term_re
                    sum_im = term_im if sum_im is None else sum_im + term_im
                if later is None:
                    out_re, out_im = sum_re, sum_im
                elif sign > 0:
                    out_re, out_im = sum_re + later[1], sum_im - later[0]
                else:
                    out_re, out_im = sum_re - later[1], sum_im + later[0]
                prod[d, at, re] = out_re.astype(BF16)
                prod[d, at, im] = out_im.astype(BF16)
                later = (sum_re, sum_im)
        return carry

    lax.fori_loop(0, rows // step, chunk, 0)


def window_kernel(rows, block, total, rates_ref, f_ref, decay, f_out):
    del f_ref, f_out
    lags = lax.broadcasted_iota(jnp.int32, (rows, block), 1) + lax.axis_index("seq") * block
    for n in range(4):
        rates = jnp.broadcast_to(rates_ref[:, n * rows : (n + 1) * rows], (block, rows)).T
        decay[n] = jnp.exp(-rates * lags.astype(F32) / total)


def filter_kernel(rows, s0, s1, s2, s3, table, back, *refs):
    outs, (spec_g, spec_z, prod) = refs[:4], refs[4:]
    me = lax.axis_index("seq")
    for k, slot in enumerate((s0, s1, s2, s3)):
        spec = dot(slot[...], table[...])
        spec_g[me ^ k] = spec[:rows]
        spec_z[me ^ k] = spec[rows:]
    correlate(rows, table.shape[0], spec_g, spec_z, prod)
    for k, out in enumerate(outs):
        out[...] = dot(prod[me ^ k], back[...]).astype(out.dtype)


def input_kernel(rows, s0, s1, s2, s3, f0, f1, f2, f3, table, back, *refs):
    outs, (spec_g, spec_z, prod) = refs[:4], refs[4:]
    me = lax.axis_index("seq")
    for k, (slot, f) in enumerate(((s0, f0), (s1, f1), (s2, f2), (s3, f3))):
        spec_g[me ^ k] = dot(slot[:rows], table[...])
        spec_z[me ^ k] = dot(f[...], table[...])
    correlate(rows, table.shape[0], spec_g, spec_z, prod)
    for k, out in enumerate(outs):
        out[...] = dot(prod[me ^ k], back[...]).astype(BF16)


def hidden_kernel(rows, w0, w1, w2, w3, decay, mix, after, filt_out, hidden, sent):
    del after
    me = lax.axis_index("seq")
    total = None
    for k, w in enumerate((w0, w1, w2, w3)):
        values = w[...].astype(F32)
        filt_out[me ^ k] = values
        windowed = values * decay[me ^ k]
        high = windowed.astype(BF16)
        low = (windowed - high.astype(F32)).astype(BF16)
        weight = mix[:, pl.ds(pl.multiple_of((me ^ k) * rows, rows), rows)]
        term = dot(weight, high) + dot(weight, low)
        total = term if total is None else total + term
    hidden[...] = total
    sent[...] = total.astype(BF16)


def final_kernel(v0, v1, v2, v3, pair, *refs):
    others, (in_out, hidden_out) = refs[:-2], refs[-2:]
    me = lax.axis_index("seq")
    for k, v in enumerate((v0, v1, v2, v3)):
        in_out[me ^ k] = v[...]
    hidden = pair[...]
    for other in others:
        hidden = hidden + other[...].astype(F32)
    hidden_out[...] = hidden


def body_four(channel_axis, inputs, grad_out, filt, rates, mix_weight):
    channels, block = inputs.shape
    rows = channels // 4
    total = 4 * block
    hidden = mix_weight.shape[1]
    forward, back = (jnp.asarray(t) for t in tables(block))
    shape = jax.ShapeDtypeStruct
    vmem = pl.BlockSpec(memory_space=pltpu.VMEM)
    params = pltpu.CompilerParams(vmem_limit_bytes=8 * 1024 * 1024)
    small = pltpu.CompilerParams(vmem_limit_bytes=4 * 1024 * 1024)
    cost = pl.CostEstimate(flops=1000, bytes_accessed=1000, transcendentals=0)
    scratch = [
        pltpu.VMEM((4, rows, 2 * block), F32),
        pltpu.VMEM((4, rows, 2 * block), F32),
        pltpu.VMEM((4, rows, 2 * block), BF16),
    ]

    me = lax.axis_index("seq")
    arrays = jnp.stack([value.reshape(4, rows, block) for value in (grad_out, inputs, filt)], 1)
    parts = [lax.dynamic_index_in_dim(arrays, me ^ k, 0, keepdims=False) for k in range(4)]
    slots = [p[:2].reshape(2 * rows, block) for p in parts]
    slots_f = [p[2] for p in parts]
    space = pl.BlockSpec(memory_space=pl.ANY)
    decay, slots_f[1] = pl.pallas_call(
        functools.partial(window_kernel, rows, block, total),
        out_shape=[shape((4, rows, block), F32), shape((rows, block), BF16)],
        in_specs=[vmem, space],
        out_specs=[vmem, space],
        input_output_aliases={1: 1},
        compiler_params=small,
        cost_estimate=cost,
    )(rates.reshape(1, channels), slots_f[1])
    slots = slots[:1] + [xor_permute(slots[k], "seq", 4, k) for k in (1, 2, 3)]
    slots_f = slots_f[:1] + [xor_permute(slots_f[k], "seq", 4, k) for k in (1, 2, 3)]

    made = pl.pallas_call(
        functools.partial(filter_kernel, rows),
        out_shape=[shape((rows, block), F32)] + [shape((rows, block), BF16)] * 3,
        in_specs=[vmem] * 6,
        out_specs=[vmem] * 4,
        scratch_shapes=scratch,
        compiler_params=params,
        cost_estimate=cost,
    )(*slots, forward, back)
    got = [xor_permute(made[k], "seq", 4, k) for k in (1, 2, 3)]

    made_in = pl.pallas_call(
        functools.partial(input_kernel, rows),
        out_shape=[shape((rows, block), BF16)] * 4,
        in_specs=[vmem] * 10,
        out_specs=[vmem] * 4,
        scratch_shapes=scratch,
        compiler_params=params,
        cost_estimate=cost,
    )(*slots, *slots_f, forward, back)
    got_in = [xor_permute(made_in[k], "seq", 4, k) for k in (1, 2, 3)]

    grad_filt, partial, partial_sent = pl.pallas_call(
        functools.partial(hidden_kernel, rows),
        out_shape=[shape((4, rows, block), F32), shape((hidden, block), F32), shape((hidden, block), BF16)],
        in_specs=[vmem] * 6 + [space],
        out_specs=[vmem] * 3,
        compiler_params=small,
        cost_estimate=cost,
    )(made[0], *got, decay, mix_weight.T, made_in[1])
    pair = partial + xor_permute(partial_sent, "chan", channel_axis, 1).astype(F32)
    pair_sent = pair.astype(BF16)
    others = [xor_permute(pair_sent, "chan", channel_axis, k) for k in range(2, channel_axis, 2)]

    grad_in, grad_hidden = pl.pallas_call(
        final_kernel,
        out_shape=[shape((4, rows, block), BF16), shape((hidden, block), F32)],
        in_specs=[vmem] * (5 + len(others)),
        out_specs=[vmem] * 2,
        compiler_params=small,
        cost_estimate=cost,
    )(made_in[0], *got_in, pair, *others)
    return grad_in.reshape(channels, block), grad_filt.reshape(channels, block), grad_hidden


def body_any(blocks, inputs, grad_out, filt, rates, mix_weight):
    channels, block = inputs.shape
    rows = channels // blocks
    total = blocks * block
    half = block // 2
    me = lax.axis_index("seq")
    forward, back = (jnp.asarray(t) for t in tables(block))
    sign = jnp.where(jnp.arange(block) < half, 1.0, -1.0).astype(F32)

    def spread(value):
        return lax.all_to_all(value.reshape(blocks, rows, block), "seq", 0, 0, tiled=True)

    def spectrum(value):
        spec = dot(value, forward)
        return spec[..., :block], spec[..., block:]

    def correlate_blocks(g, z):
        sums = []
        for d in range(blocks):
            gr, gi, zr, zi = g[0][d:], g[1][d:], z[0][: blocks - d], z[1][: blocks - d]
            sums.append(((gr * zr + gi * zi).sum(0), (gi * zr - gr * zi).sum(0)))
        sums.append((jnp.zeros_like(sums[0][0]),) * 2)
        out = [
            jnp.concatenate([sums[d][0] + sign * sums[d + 1][1], sums[d][1] - sign * sums[d + 1][0]], axis=-1)
            for d in range(blocks)
        ]
        return dot(jnp.stack(out).astype(BF16), back)

    spec_g = spectrum(spread(grad_out))
    grad_filt = correlate_blocks(spec_g, spectrum(spread(inputs)))
    grad_in = correlate_blocks(spec_g, spectrum(spread(filt)))
    grad_in = spread(grad_in.astype(BF16)).reshape(channels, block)
    grad_filt = lax.all_to_all(grad_filt, "seq", 0, 0, tiled=True).reshape(channels, block)
    lags = (me * block + jnp.arange(block, dtype=jnp.int32)).astype(F32)
    windowed = grad_filt * jnp.exp(-rates[:, None] * lags[None, :] / total)
    high = windowed.astype(BF16)
    low = (windowed - high.astype(F32)).astype(BF16)
    grad_hidden = lax.psum(dot(mix_weight.T, high) + dot(mix_weight.T, low), "chan")
    return grad_in, grad_filt, grad_hidden


def solution(mesh):
    blocks, chan = mesh.shape["seq"], mesh.shape["chan"]

    def body(inputs, grad_out, filt, rates, mix_weight):
        if blocks == 4 and chan & (chan - 1) == 0 and inputs.shape[0] % 512 == 0 and inputs.shape[1] % 256 == 0:
            return body_four(chan, inputs, grad_out, filt, rates, mix_weight)
        return body_any(blocks, inputs, grad_out, filt, rates, mix_weight)

    return jax.shard_map(
        body,
        mesh=mesh,
        in_specs=(P("chan", "seq"), P("chan", "seq"), P("chan", "seq"), P("chan"), P("chan", None)),
        out_specs=(P("chan", "seq"), P("chan", "seq"), P(None, "seq")),
        check_vma=False,
    )
```

```python
import functools

import jax
import jax.numpy as jnp
import ml_dtypes
import numpy as np
from jax import lax
from jax.experimental import pallas as pl
from jax.experimental.pallas import tpu as pltpu
from jax.sharding import PartitionSpec as P

F32 = jnp.float32
BF16 = jnp.bfloat16


def tables(block):
    k = np.concatenate([np.arange(0, block, 2), np.arange(1, block, 2)]).astype(np.float64)
    phase = np.pi * (k[None, :] + 0.5) * np.arange(block, dtype=np.float64)[:, None] / block
    forward = np.concatenate([np.cos(phase), -np.sin(phase)], axis=1)
    back = forward.T / block
    return forward.astype(ml_dtypes.bfloat16), back.astype(ml_dtypes.bfloat16)


def dot(left, right):
    return jnp.dot(left, right, preferred_element_type=F32)


def xor_permute(value, axis, size, k):
    return lax.ppermute(value, axis, [(j, j ^ k) for j in range(size)])


def correlate(rows, block, spec_g, spec_z, prod):
    half = block // 2
    step = 16

    def chunk(c, carry):
        at = pl.ds(pl.multiple_of(c * step, step), step)
        for part, sign in ((0, 1.0), (1, -1.0)):
            re = pl.ds(part * half, half)
            im = pl.ds(block + part * half, half)
            g = [(spec_g[j, at, re], spec_g[j, at, im]) for j in range(4)]
            z = [(spec_z[j, at, re], spec_z[j, at, im]) for j in range(4)]
            later = None
            for d in (3, 2, 1, 0):
                sum_re = sum_im = None
                for j in range(d, 4):
                    gr, gi = g[j]
                    zr, zi = z[j - d]
                    term_re = gr * zr + gi * zi
                    term_im = gi * zr - gr * zi
                    sum_re = term_re if sum_re is None else sum_re + term_re
                    sum_im = term_im if sum_im is None else sum_im + term_im
                if later is None:
                    out_re, out_im = sum_re, sum_im
                elif sign > 0:
                    out_re, out_im = sum_re + later[1], sum_im - later[0]
                else:
                    out_re, out_im = sum_re - later[1], sum_im + later[0]
                prod[d, at, re] = out_re.astype(BF16)
                prod[d, at, im] = out_im.astype(BF16)
                later = (sum_re, sum_im)
        return carry

    lax.fori_loop(0, rows // step, chunk, 0)


def window_kernel(rows, block, total, rates_ref, f_ref, decay, f_out):
    del f_ref, f_out
    lags = lax.broadcasted_iota(jnp.int32, (rows, block), 1) + lax.axis_index("seq") * block
    for n in range(4):
        rates = jnp.broadcast_to(rates_ref[:, n * rows : (n + 1) * rows], (block, rows)).T
        decay[n] = jnp.exp(-rates * lags.astype(F32) / total)


def filter_kernel(rows, s0, s1, s2, s3, table, back, *refs):
    outs, (spec_g, spec_z, prod) = refs[:4], refs[4:]
    me = lax.axis_index("seq")
    for k, slot in enumerate((s0, s1, s2, s3)):
        spec = dot(slot[...], table[...])
        spec_g[me ^ k] = spec[:rows]
        spec_z[me ^ k] = spec[rows:]
    correlate(rows, table.shape[0], spec_g, spec_z, prod)
    for k, out in enumerate(outs):
        out[...] = dot(prod[me ^ k], back[...]).astype(out.dtype)


def input_kernel(rows, s0, s1, s2, s3, f0, f1, f2, f3, table, back, *refs):
    outs, (spec_g, spec_z, prod) = refs[:4], refs[4:]
    me = lax.axis_index("seq")
    for k, (slot, f) in enumerate(((s0, f0), (s1, f1), (s2, f2), (s3, f3))):
        spec_g[me ^ k] = dot(slot[:rows], table[...])
        spec_z[me ^ k] = dot(f[...], table[...])
    correlate(rows, table.shape[0], spec_g, spec_z, prod)
    for k, out in enumerate(outs):
        out[...] = dot(prod[me ^ k], back[...])


def hidden_kernel(rows, w0, w1, w2, w3, decay, mix, after, hidden, sent):
    del after
    me = lax.axis_index("seq")
    total = None
    for k, w in enumerate((w0, w1, w2, w3)):
        windowed = w[...].astype(F32) * decay[me ^ k]
        high = windowed.astype(BF16)
        low = (windowed - high.astype(F32)).astype(BF16)
        weight = mix[:, pl.ds(pl.multiple_of((me ^ k) * rows, rows), rows)]
        term = dot(weight, high) + dot(weight, low)
        total = term if total is None else total + term
    hidden[...] = total
    sent[...] = total.astype(BF16)


def unpack_kernel(w0, w1, w2, w3, filt_out, token):
    me = lax.axis_index("seq")
    for k, w in enumerate((w0, w1, w2, w3)):
        filt_out[me ^ k] = w[...].astype(F32)
    token[...] = jnp.zeros_like(token)


def pair_kernel(own, other, out, sent):
    total = own[...] + other[...].astype(F32)
    out[...] = total
    sent[...] = total.astype(BF16)


def sum_kernel(pair, first, second, token, out, sent):
    del token
    lead = lax.axis_index("chan") % 2 == 1
    total = first[...].astype(F32) + jnp.where(lead, second[...].astype(F32), pair[...])
    out[...] = total
    sent[...] = total.astype(BF16)


def final_kernel(v0, v1, v2, v3, own, other, in_out, hidden_out):
    me = lax.axis_index("seq")
    for k, v in enumerate((v0, v1, v2, v3)):
        in_out[me ^ k] = v[...].astype(BF16)
    hidden_out[...] = own[...] + other[...].astype(F32)


def body_four(channel_axis, inputs, grad_out, filt, rates, mix_weight):
    channels, block = inputs.shape
    rows = channels // 4
    total = 4 * block
    hidden = mix_weight.shape[1]
    forward, back = (jnp.asarray(t) for t in tables(block))
    shape = jax.ShapeDtypeStruct
    vmem = pl.BlockSpec(memory_space=pltpu.VMEM)
    params = pltpu.CompilerParams(vmem_limit_bytes=8 * 1024 * 1024)
    small = pltpu.CompilerParams(vmem_limit_bytes=4 * 1024 * 1024)
    cost = pl.CostEstimate(flops=1000, bytes_accessed=1000, transcendentals=0)
    scratch = [
        pltpu.VMEM((4, rows, 2 * block), F32),
        pltpu.VMEM((4, rows, 2 * block), F32),
        pltpu.VMEM((4, rows, 2 * block), BF16),
    ]

    me = lax.axis_index("seq")
    arrays = jnp.stack([value.reshape(4, rows, block) for value in (grad_out, inputs)], 1)
    slots = [lax.dynamic_index_in_dim(arrays, me ^ k, 0, keepdims=False).reshape(2 * rows, block) for k in range(4)]
    slots_f = [lax.dynamic_index_in_dim(filt.reshape(4, rows, block), me ^ k, 0, keepdims=False) for k in range(4)]
    space = pl.BlockSpec(memory_space=pl.ANY)
    decay, slots_f[1] = pl.pallas_call(
        functools.partial(window_kernel, rows, block, total),
        out_shape=[shape((4, rows, block), F32), shape((rows, block), BF16)],
        in_specs=[vmem, space],
        out_specs=[vmem, space],
        input_output_aliases={1: 1},
        compiler_params=small,
        cost_estimate=cost,
    )(rates.reshape(1, channels), slots_f[1])
    slots = slots[:1] + [xor_permute(slots[k], "seq", 4, k) for k in (1, 2, 3)]
    slots_f = slots_f[:1] + [xor_permute(slots_f[k], "seq", 4, k) for k in (1, 2, 3)]

    made = pl.pallas_call(
        functools.partial(filter_kernel, rows),
        out_shape=[shape((rows, block), F32)] + [shape((rows, block), BF16)] * 3,
        in_specs=[vmem] * 6,
        out_specs=[vmem] * 4,
        scratch_shapes=scratch,
        compiler_params=params,
        cost_estimate=cost,
    )(*slots, forward, back)
    got = [xor_permute(made[k], "seq", 4, k) for k in (1, 2, 3)]

    made_in = pl.pallas_call(
        functools.partial(input_kernel, rows),
        out_shape=[shape((rows, block), F32)] * 4,
        in_specs=[vmem] * 10,
        out_specs=[vmem] * 4,
        scratch_shapes=scratch,
        compiler_params=params,
        cost_estimate=cost,
    )(*slots, *slots_f, forward, back)
    got_in = [xor_permute(made_in[k], "seq", 4, k) for k in (1, 2, 3)]

    partial, partial_sent = pl.pallas_call(
        functools.partial(hidden_kernel, rows),
        out_shape=[shape((hidden, block), F32), shape((hidden, block), BF16)],
        in_specs=[vmem] * 6 + [space],
        out_specs=[vmem] * 2,
        compiler_params=small,
        cost_estimate=cost,
    )(made[0], *got, decay, mix_weight.T, made_in[1])
    grad_filt, token = pl.pallas_call(
        unpack_kernel,
        out_shape=[shape((4, rows, block), F32), shape((8, 128), F32)],
        in_specs=[vmem] * 4,
        out_specs=[vmem] * 2,
        compiler_params=small,
        cost_estimate=cost,
    )(made[0], *got)
    pair, pair_sent = pl.pallas_call(
        pair_kernel,
        out_shape=[shape((hidden, block), F32), shape((hidden, block), BF16)],
        in_specs=[vmem] * 2,
        out_specs=[vmem] * 2,
        compiler_params=small,
        cost_estimate=cost,
    )(partial, xor_permute(partial_sent, "chan", channel_axis, 1))
    first = lax.ppermute(pair_sent, "chan", [(c, c ^ (4 if c % 2 else 6)) for c in range(channel_axis)])
    second = lax.ppermute(pair_sent, "chan", [(c, c ^ (2 if c % 2 else 0)) for c in range(channel_axis)])
    half_sum, half_sent = pl.pallas_call(
        sum_kernel,
        out_shape=[shape((hidden, block), F32), shape((hidden, block), BF16)],
        in_specs=[vmem] * 3 + [space],
        out_specs=[vmem] * 2,
        compiler_params=small,
        cost_estimate=cost,
    )(pair, first, second, token)
    other_half = xor_permute(half_sent, "chan", channel_axis, 1)

    grad_in, grad_hidden = pl.pallas_call(
        final_kernel,
        out_shape=[shape((4, rows, block), BF16), shape((hidden, block), F32)],
        in_specs=[vmem] * 6,
        out_specs=[vmem] * 2,
        compiler_params=small,
        cost_estimate=cost,
    )(made_in[0], *got_in, half_sum, other_half)
    return grad_in.reshape(channels, block), grad_filt.reshape(channels, block), grad_hidden


def body_any(blocks, inputs, grad_out, filt, rates, mix_weight):
    channels, block = inputs.shape
    rows = channels // blocks
    total = blocks * block
    half = block // 2
    me = lax.axis_index("seq")
    forward, back = (jnp.asarray(t) for t in tables(block))
    sign = jnp.where(jnp.arange(block) < half, 1.0, -1.0).astype(F32)

    def spread(value):
        return lax.all_to_all(value.reshape(blocks, rows, block), "seq", 0, 0, tiled=True)

    def spectrum(value):
        spec = dot(value, forward)
        return spec[..., :block], spec[..., block:]

    def correlate_blocks(g, z):
        sums = []
        for d in range(blocks):
            gr, gi, zr, zi = g[0][d:], g[1][d:], z[0][: blocks - d], z[1][: blocks - d]
            sums.append(((gr * zr + gi * zi).sum(0), (gi * zr - gr * zi).sum(0)))
        sums.append((jnp.zeros_like(sums[0][0]),) * 2)
        out = [
            jnp.concatenate([sums[d][0] + sign * sums[d + 1][1], sums[d][1] - sign * sums[d + 1][0]], axis=-1)
            for d in range(blocks)
        ]
        return dot(jnp.stack(out).astype(BF16), back)

    spec_g = spectrum(spread(grad_out))
    grad_filt = correlate_blocks(spec_g, spectrum(spread(inputs)))
    grad_in = correlate_blocks(spec_g, spectrum(spread(filt)))
    grad_in = spread(grad_in.astype(BF16)).reshape(channels, block)
    grad_filt = lax.all_to_all(grad_filt, "seq", 0, 0, tiled=True).reshape(channels, block)
    lags = (me * block + jnp.arange(block, dtype=jnp.int32)).astype(F32)
    windowed = grad_filt * jnp.exp(-rates[:, None] * lags[None, :] / total)
    high = windowed.astype(BF16)
    low = (windowed - high.astype(F32)).astype(BF16)
    grad_hidden = lax.psum(dot(mix_weight.T, high) + dot(mix_weight.T, low), "chan")
    return grad_in, grad_filt, grad_hidden


def solution(mesh):
    blocks, chan = mesh.shape["seq"], mesh.shape["chan"]

    def body(inputs, grad_out, filt, rates, mix_weight):
        if blocks == 4 and chan & (chan - 1) == 0 and inputs.shape[0] % 512 == 0 and inputs.shape[1] % 256 == 0:
            return body_four(chan, inputs, grad_out, filt, rates, mix_weight)
        return body_any(blocks, inputs, grad_out, filt, rates, mix_weight)

    return jax.shard_map(
        body,
        mesh=mesh,
        in_specs=(P("chan", "seq"), P("chan", "seq"), P("chan", "seq"), P("chan"), P("chan", None)),
        out_specs=(P("chan", "seq"), P("chan", "seq"), P(None, "seq")),
        check_vma=False,
    )
```

```python
import functools

import jax
import jax.numpy as jnp
import ml_dtypes
import numpy as np
from jax import lax
from jax.experimental import pallas as pl
from jax.experimental.pallas import tpu as pltpu
from jax.sharding import PartitionSpec as P

F32 = jnp.float32
BF16 = jnp.bfloat16


def tables(block):
    k = np.concatenate([np.arange(0, block, 2), np.arange(1, block, 2)]).astype(np.float64)
    phase = np.pi * (k[None, :] + 0.5) * np.arange(block, dtype=np.float64)[:, None] / block
    forward = np.concatenate([np.cos(phase), -np.sin(phase)], axis=1)
    back = forward.T / block
    return forward.astype(ml_dtypes.bfloat16), back.astype(ml_dtypes.bfloat16)


def dot(left, right):
    return jnp.dot(left, right, preferred_element_type=F32)


def xor_permute(value, axis, size, k):
    return lax.ppermute(value, axis, [(j, j ^ k) for j in range(size)])


def correlate(rows, block, spec_g, spec_z, prod):
    half = block // 2
    step = 16

    def chunk(c, carry):
        at = pl.ds(pl.multiple_of(c * step, step), step)
        for part, sign in ((0, 1.0), (1, -1.0)):
            re = pl.ds(part * half, half)
            im = pl.ds(block + part * half, half)
            g = [(spec_g[j, at, re], spec_g[j, at, im]) for j in range(4)]
            z = [(spec_z[j, at, re], spec_z[j, at, im]) for j in range(4)]
            later = None
            for d in (3, 2, 1, 0):
                sum_re = sum_im = None
                for j in range(d, 4):
                    gr, gi = g[j]
                    zr, zi = z[j - d]
                    term_re = gr * zr + gi * zi
                    term_im = gi * zr - gr * zi
                    sum_re = term_re if sum_re is None else sum_re + term_re
                    sum_im = term_im if sum_im is None else sum_im + term_im
                if later is None:
                    out_re, out_im = sum_re, sum_im
                elif sign > 0:
                    out_re, out_im = sum_re + later[1], sum_im - later[0]
                else:
                    out_re, out_im = sum_re - later[1], sum_im + later[0]
                prod[d, at, re] = out_re.astype(BF16)
                prod[d, at, im] = out_im.astype(BF16)
                later = (sum_re, sum_im)
        return carry

    lax.fori_loop(0, rows // step, chunk, 0)


def window_kernel(rows, block, total, rates_ref, f_ref, decay, f_out):
    del f_ref, f_out
    lags = lax.broadcasted_iota(jnp.int32, (rows, block), 1) + lax.axis_index("seq") * block
    for n in range(4):
        rates = jnp.broadcast_to(rates_ref[:, n * rows : (n + 1) * rows], (block, rows)).T
        decay[n] = jnp.exp(-rates * lags.astype(F32) / total)


def filter_kernel(rows, s0, s1, s2, s3, table, back, *refs):
    outs, (spec_g, spec_z, prod) = refs[:4], refs[4:]
    me = lax.axis_index("seq")
    for k, slot in enumerate((s0, s1, s2, s3)):
        spec = dot(slot[...], table[...])
        spec_g[me ^ k] = spec[:rows]
        spec_z[me ^ k] = spec[rows:]
    correlate(rows, table.shape[0], spec_g, spec_z, prod)
    for k, out in enumerate(outs):
        out[...] = dot(prod[me ^ k], back[...]).astype(out.dtype)


def input_kernel(rows, s0, s1, s2, s3, f0, f1, f2, f3, table, back, *refs):
    outs, (spec_g, spec_z, prod) = refs[:4], refs[4:]
    me = lax.axis_index("seq")
    for k, (slot, f) in enumerate(((s0, f0), (s1, f1), (s2, f2), (s3, f3))):
        spec_g[me ^ k] = dot(slot[:rows], table[...])
        spec_z[me ^ k] = dot(f[...], table[...])
    correlate(rows, table.shape[0], spec_g, spec_z, prod)
    for k, out in enumerate(outs):
        out[...] = dot(prod[me ^ k], back[...])


def hidden_kernel(rows, w0, w1, w2, w3, decay, mix, after, hidden, sent):
    del after
    me = lax.axis_index("seq")
    total = None
    for k, w in enumerate((w0, w1, w2, w3)):
        windowed = w[...].astype(F32) * decay[me ^ k]
        high = windowed.astype(BF16)
        low = (windowed - high.astype(F32)).astype(BF16)
        weight = mix[:, pl.ds(pl.multiple_of((me ^ k) * rows, rows), rows)]
        term = dot(weight, high) + dot(weight, low)
        total = term if total is None else total + term
    hidden[...] = total
    sent[...] = total.astype(BF16)


def unpack_kernel(w0, w1, w2, w3, filt_out, token):
    me = lax.axis_index("seq")
    for k, w in enumerate((w0, w1, w2, w3)):
        filt_out[me ^ k] = w[...].astype(F32)
    token[...] = jnp.zeros_like(token)


def pair_kernel(own, other, out, sent):
    total = own[...] + other[...].astype(F32)
    out[...] = total
    sent[...] = total.astype(BF16)


def sum_kernel(pair, first, second, token, out, sent):
    del token
    lead = lax.axis_index("chan") % 2 == 1
    total = first[...].astype(F32) + jnp.where(lead, second[...].astype(F32), pair[...])
    out[...] = total
    sent[...] = total.astype(BF16)


def final_kernel(v0, v1, v2, v3, own, other, in_out, hidden_out):
    me = lax.axis_index("seq")
    for k, v in enumerate((v0, v1, v2, v3)):
        in_out[me ^ k] = v[...].astype(BF16)
    hidden_out[...] = own[...] + other[...].astype(F32)


def body_four(channel_axis, inputs, grad_out, filt, rates, mix_weight):
    channels, block = inputs.shape
    rows = channels // 4
    total = 4 * block
    hidden = mix_weight.shape[1]
    forward, back = (jnp.asarray(t) for t in tables(block))
    shape = jax.ShapeDtypeStruct
    vmem = pl.BlockSpec(memory_space=pltpu.VMEM)
    params = pltpu.CompilerParams(vmem_limit_bytes=8 * 1024 * 1024)
    small = pltpu.CompilerParams(vmem_limit_bytes=4 * 1024 * 1024)
    cost = pl.CostEstimate(flops=1000, bytes_accessed=1000, transcendentals=0)
    scratch = [
        pltpu.VMEM((4, rows, 2 * block), F32),
        pltpu.VMEM((4, rows, 2 * block), F32),
        pltpu.VMEM((4, rows, 2 * block), BF16),
    ]

    me = lax.axis_index("seq")
    arrays = jnp.stack([value.reshape(4, rows, block) for value in (grad_out, inputs)], 1)
    slots = [lax.dynamic_index_in_dim(arrays, me ^ k, 0, keepdims=False).reshape(2 * rows, block) for k in range(4)]
    slots_f = [lax.dynamic_index_in_dim(filt.reshape(4, rows, block), me ^ k, 0, keepdims=False) for k in range(4)]
    space = pl.BlockSpec(memory_space=pl.ANY)
    decay, slots_f[1] = pl.pallas_call(
        functools.partial(window_kernel, rows, block, total),
        out_shape=[shape((4, rows, block), F32), shape((rows, block), BF16)],
        in_specs=[vmem, space],
        out_specs=[vmem, space],
        input_output_aliases={1: 1},
        compiler_params=pltpu.CompilerParams(vmem_limit_bytes=60 * 1024 * 1024),
        cost_estimate=cost,
    )(rates.reshape(1, channels), slots_f[1])
    slots = slots[:1] + [xor_permute(slots[k], "seq", 4, k) for k in (1, 2, 3)]
    slots_f = slots_f[:1] + [xor_permute(slots_f[k], "seq", 4, k) for k in (1, 2, 3)]

    made = pl.pallas_call(
        functools.partial(filter_kernel, rows),
        out_shape=[shape((rows, block), F32)] + [shape((rows, block), BF16)] * 3,
        in_specs=[vmem] * 6,
        out_specs=[vmem] * 4,
        scratch_shapes=scratch,
        compiler_params=params,
        cost_estimate=cost,
    )(*slots, forward, back)
    got = [xor_permute(made[k], "seq", 4, k) for k in (1, 2, 3)]

    made_in = pl.pallas_call(
        functools.partial(input_kernel, rows),
        out_shape=[shape((rows, block), F32)] * 4,
        in_specs=[vmem] * 10,
        out_specs=[vmem] * 4,
        scratch_shapes=scratch,
        compiler_params=params,
        cost_estimate=cost,
    )(*slots, *slots_f, forward, back)
    got_in = [xor_permute(made_in[k], "seq", 4, k) for k in (1, 2, 3)]

    partial, partial_sent = pl.pallas_call(
        functools.partial(hidden_kernel, rows),
        out_shape=[shape((hidden, block), F32), shape((hidden, block), BF16)],
        in_specs=[vmem] * 6 + [space],
        out_specs=[vmem] * 2,
        compiler_params=small,
        cost_estimate=cost,
    )(made[0], *got, decay, mix_weight.T, made_in[1])
    grad_filt, token = pl.pallas_call(
        unpack_kernel,
        out_shape=[shape((4, rows, block), F32), shape((8, 128), F32)],
        in_specs=[vmem] * 4,
        out_specs=[vmem] * 2,
        compiler_params=small,
        cost_estimate=cost,
    )(made[0], *got)
    pair, pair_sent = pl.pallas_call(
        pair_kernel,
        out_shape=[shape((hidden, block), F32), shape((hidden, block), BF16)],
        in_specs=[vmem] * 2,
        out_specs=[vmem] * 2,
        compiler_params=small,
        cost_estimate=cost,
    )(partial, xor_permute(partial_sent, "chan", channel_axis, 1))
    first = lax.ppermute(pair_sent, "chan", [(c, c ^ (4 if c % 2 else 6)) for c in range(channel_axis)])
    second = lax.ppermute(pair_sent, "chan", [(c, c ^ (2 if c % 2 else 0)) for c in range(channel_axis)])
    half_sum, half_sent = pl.pallas_call(
        sum_kernel,
        out_shape=[shape((hidden, block), F32), shape((hidden, block), BF16)],
        in_specs=[vmem] * 3 + [space],
        out_specs=[vmem] * 2,
        compiler_params=small,
        cost_estimate=cost,
    )(pair, first, second, token)
    other_half = xor_permute(half_sent, "chan", channel_axis, 1)

    grad_in, grad_hidden = pl.pallas_call(
        final_kernel,
        out_shape=[shape((4, rows, block), BF16), shape((hidden, block), F32)],
        in_specs=[vmem] * 6,
        out_specs=[vmem] * 2,
        compiler_params=small,
        cost_estimate=cost,
    )(made_in[0], *got_in, half_sum, other_half)
    return grad_in.reshape(channels, block), grad_filt.reshape(channels, block), grad_hidden


def body_any(blocks, inputs, grad_out, filt, rates, mix_weight):
    channels, block = inputs.shape
    rows = channels // blocks
    total = blocks * block
    half = block // 2
    me = lax.axis_index("seq")
    forward, back = (jnp.asarray(t) for t in tables(block))
    sign = jnp.where(jnp.arange(block) < half, 1.0, -1.0).astype(F32)

    def spread(value):
        return lax.all_to_all(value.reshape(blocks, rows, block), "seq", 0, 0, tiled=True)

    def spectrum(value):
        spec = dot(value, forward)
        return spec[..., :block], spec[..., block:]

    def correlate_blocks(g, z):
        sums = []
        for d in range(blocks):
            gr, gi, zr, zi = g[0][d:], g[1][d:], z[0][: blocks - d], z[1][: blocks - d]
            sums.append(((gr * zr + gi * zi).sum(0), (gi * zr - gr * zi).sum(0)))
        sums.append((jnp.zeros_like(sums[0][0]),) * 2)
        out = [
            jnp.concatenate([sums[d][0] + sign * sums[d + 1][1], sums[d][1] - sign * sums[d + 1][0]], axis=-1)
            for d in range(blocks)
        ]
        return dot(jnp.stack(out).astype(BF16), back)

    spec_g = spectrum(spread(grad_out))
    grad_filt = correlate_blocks(spec_g, spectrum(spread(inputs)))
    grad_in = correlate_blocks(spec_g, spectrum(spread(filt)))
    grad_in = spread(grad_in.astype(BF16)).reshape(channels, block)
    grad_filt = lax.all_to_all(grad_filt, "seq", 0, 0, tiled=True).reshape(channels, block)
    lags = (me * block + jnp.arange(block, dtype=jnp.int32)).astype(F32)
    windowed = grad_filt * jnp.exp(-rates[:, None] * lags[None, :] / total)
    high = windowed.astype(BF16)
    low = (windowed - high.astype(F32)).astype(BF16)
    grad_hidden = lax.psum(dot(mix_weight.T, high) + dot(mix_weight.T, low), "chan")
    return grad_in, grad_filt, grad_hidden


def solution(mesh):
    blocks, chan = mesh.shape["seq"], mesh.shape["chan"]

    def body(inputs, grad_out, filt, rates, mix_weight):
        if blocks == 4 and chan & (chan - 1) == 0 and inputs.shape[0] % 512 == 0 and inputs.shape[1] % 256 == 0:
            return body_four(chan, inputs, grad_out, filt, rates, mix_weight)
        return body_any(blocks, inputs, grad_out, filt, rates, mix_weight)

    return jax.shard_map(
        body,
        mesh=mesh,
        in_specs=(P("chan", "seq"), P("chan", "seq"), P("chan", "seq"), P("chan"), P("chan", None)),
        out_specs=(P("chan", "seq"), P("chan", "seq"), P(None, "seq")),
        check_vma=False,
    )
```

```python
import functools

import jax
import jax.numpy as jnp
import ml_dtypes
import numpy as np
from jax import lax
from jax.experimental import pallas as pl
from jax.experimental.pallas import tpu as pltpu
from jax.sharding import PartitionSpec as P

F32 = jnp.float32
BF16 = jnp.bfloat16


def tables(block):
    k = np.concatenate([np.arange(0, block, 2), np.arange(1, block, 2)]).astype(np.float64)
    phase = np.pi * (k[None, :] + 0.5) * np.arange(block, dtype=np.float64)[:, None] / block
    forward = np.concatenate([np.cos(phase), -np.sin(phase)], axis=1)
    back = forward.T / block
    return forward.astype(ml_dtypes.bfloat16), back.astype(ml_dtypes.bfloat16)


def dot(left, right):
    return jnp.dot(left, right, preferred_element_type=F32)


def xor_permute(value, axis, size, k):
    return lax.ppermute(value, axis, [(j, j ^ k) for j in range(size)])


def correlate(rows, block, spec_g, spec_z, prod):
    half = block // 2
    step = 16

    def chunk(c, carry):
        at = pl.ds(pl.multiple_of(c * step, step), step)
        for part, sign in ((0, 1.0), (1, -1.0)):
            re = pl.ds(part * half, half)
            im = pl.ds(block + part * half, half)
            g = [(spec_g[j, at, re], spec_g[j, at, im]) for j in range(4)]
            z = [(spec_z[j, at, re], spec_z[j, at, im]) for j in range(4)]
            later = None
            for d in (3, 2, 1, 0):
                sum_re = sum_im = None
                for j in range(d, 4):
                    gr, gi = g[j]
                    zr, zi = z[j - d]
                    term_re = gr * zr + gi * zi
                    term_im = gi * zr - gr * zi
                    sum_re = term_re if sum_re is None else sum_re + term_re
                    sum_im = term_im if sum_im is None else sum_im + term_im
                if later is None:
                    out_re, out_im = sum_re, sum_im
                elif sign > 0:
                    out_re, out_im = sum_re + later[1], sum_im - later[0]
                else:
                    out_re, out_im = sum_re - later[1], sum_im + later[0]
                prod[d, at, re] = out_re.astype(BF16)
                prod[d, at, im] = out_im.astype(BF16)
                later = (sum_re, sum_im)
        return carry

    lax.fori_loop(0, rows // step, chunk, 0, unroll=True)


def window_kernel(rows, block, total, rates_ref, f_ref, decay, f_out):
    del f_ref, f_out
    lags = lax.broadcasted_iota(jnp.int32, (rows, block), 1) + lax.axis_index("seq") * block
    for n in range(4):
        rates = jnp.broadcast_to(rates_ref[:, n * rows : (n + 1) * rows], (block, rows)).T
        decay[n] = jnp.exp(-rates * lags.astype(F32) / total)


def filter_kernel(rows, s0, s1, s2, s3, table, back, *refs):
    outs, (spec_g, spec_z, prod) = refs[:4], refs[4:]
    me = lax.axis_index("seq")
    for k, slot in enumerate((s0, s1, s2, s3)):
        spec = dot(slot[...], table[...])
        spec_g[me ^ k] = spec[:rows]
        spec_z[me ^ k] = spec[rows:]
    correlate(rows, table.shape[0], spec_g, spec_z, prod)
    for k, out in enumerate(outs):
        out[...] = dot(prod[me ^ k], back[...]).astype(out.dtype)


def input_kernel(rows, s0, s1, s2, s3, f0, f1, f2, f3, table, back, *refs):
    outs, (spec_g, spec_z, prod) = refs[:4], refs[4:]
    me = lax.axis_index("seq")
    for k, (slot, f) in enumerate(((s0, f0), (s1, f1), (s2, f2), (s3, f3))):
        spec_g[me ^ k] = dot(slot[:rows], table[...])
        spec_z[me ^ k] = dot(f[...], table[...])
    correlate(rows, table.shape[0], spec_g, spec_z, prod)
    for k, out in enumerate(outs):
        out[...] = dot(prod[me ^ k], back[...])


def hidden_kernel(rows, w0, w1, w2, w3, decay, mix, after, hidden, sent):
    del after
    me = lax.axis_index("seq")
    total = None
    for k, w in enumerate((w0, w1, w2, w3)):
        windowed = w[...].astype(F32) * decay[me ^ k]
        high = windowed.astype(BF16)
        low = (windowed - high.astype(F32)).astype(BF16)
        weight = mix[:, pl.ds(pl.multiple_of((me ^ k) * rows, rows), rows)]
        term = dot(weight, high) + dot(weight, low)
        total = term if total is None else total + term
    hidden[...] = total
    sent[...] = total.astype(BF16)


def unpack_kernel(w0, w1, w2, w3, filt_out, token):
    me = lax.axis_index("seq")
    for k, w in enumerate((w0, w1, w2, w3)):
        filt_out[me ^ k] = w[...].astype(F32)
    token[...] = jnp.zeros_like(token)


def pair_kernel(own, other, out, sent):
    total = own[...] + other[...].astype(F32)
    out[...] = total
    sent[...] = total.astype(BF16)


def sum_kernel(pair, first, second, token, out, sent):
    del token
    lead = lax.axis_index("chan") % 2 == 1
    total = first[...].astype(F32) + jnp.where(lead, second[...].astype(F32), pair[...])
    out[...] = total
    sent[...] = total.astype(BF16)


def final_kernel(v0, v1, v2, v3, own, other, in_out, hidden_out):
    me = lax.axis_index("seq")
    for k, v in enumerate((v0, v1, v2, v3)):
        in_out[me ^ k] = v[...].astype(BF16)
    hidden_out[...] = own[...] + other[...].astype(F32)


def body_four(channel_axis, inputs, grad_out, filt, rates, mix_weight):
    channels, block = inputs.shape
    rows = channels // 4
    total = 4 * block
    hidden = mix_weight.shape[1]
    forward, back = (jnp.asarray(t) for t in tables(block))
    shape = jax.ShapeDtypeStruct
    vmem = pl.BlockSpec(memory_space=pltpu.VMEM)
    params = pltpu.CompilerParams(vmem_limit_bytes=8 * 1024 * 1024)
    small = pltpu.CompilerParams(vmem_limit_bytes=4 * 1024 * 1024)
    cost = pl.CostEstimate(flops=1000, bytes_accessed=1000, transcendentals=0)
    scratch = [
        pltpu.VMEM((4, rows, 2 * block), F32),
        pltpu.VMEM((4, rows, 2 * block), F32),
        pltpu.VMEM((4, rows, 2 * block), BF16),
    ]

    me = lax.axis_index("seq")
    arrays = jnp.stack([value.reshape(4, rows, block) for value in (grad_out, inputs)], 1)
    slots = [lax.dynamic_index_in_dim(arrays, me ^ k, 0, keepdims=False).reshape(2 * rows, block) for k in range(4)]
    slots_f = [lax.dynamic_index_in_dim(filt.reshape(4, rows, block), me ^ k, 0, keepdims=False) for k in range(4)]
    space = pl.BlockSpec(memory_space=pl.ANY)
    decay, slots_f[1] = pl.pallas_call(
        functools.partial(window_kernel, rows, block, total),
        out_shape=[shape((4, rows, block), F32), shape((rows, block), BF16)],
        in_specs=[vmem, space],
        out_specs=[vmem, space],
        input_output_aliases={1: 1},
        compiler_params=pltpu.CompilerParams(vmem_limit_bytes=60 * 1024 * 1024),
        cost_estimate=cost,
    )(rates.reshape(1, channels), slots_f[1])
    slots = slots[:1] + [xor_permute(slots[k], "seq", 4, k) for k in (1, 2, 3)]
    slots_f = slots_f[:1] + [xor_permute(slots_f[k], "seq", 4, k) for k in (1, 2, 3)]

    made = pl.pallas_call(
        functools.partial(filter_kernel, rows),
        out_shape=[shape((rows, block), F32)] + [shape((rows, block), BF16)] * 3,
        in_specs=[vmem] * 6,
        out_specs=[vmem] * 4,
        scratch_shapes=scratch,
        compiler_params=params,
        cost_estimate=cost,
    )(*slots, forward, back)
    got = [xor_permute(made[k], "seq", 4, k) for k in (1, 2, 3)]

    made_in = pl.pallas_call(
        functools.partial(input_kernel, rows),
        out_shape=[shape((rows, block), F32)] * 4,
        in_specs=[vmem] * 10,
        out_specs=[vmem] * 4,
        scratch_shapes=scratch,
        compiler_params=params,
        cost_estimate=cost,
    )(*slots, *slots_f, forward, back)
    got_in = [xor_permute(made_in[k], "seq", 4, k) for k in (1, 2, 3)]

    partial, partial_sent = pl.pallas_call(
        functools.partial(hidden_kernel, rows),
        out_shape=[shape((hidden, block), F32), shape((hidden, block), BF16)],
        in_specs=[vmem] * 6 + [space],
        out_specs=[vmem] * 2,
        compiler_params=small,
        cost_estimate=cost,
    )(made[0], *got, decay, mix_weight.T, made_in[1])
    grad_filt, token = pl.pallas_call(
        unpack_kernel,
        out_shape=[shape((4, rows, block), F32), shape((8, 128), F32)],
        in_specs=[vmem] * 4,
        out_specs=[vmem] * 2,
        compiler_params=small,
        cost_estimate=cost,
    )(made[0], *got)
    pair, pair_sent = pl.pallas_call(
        pair_kernel,
        out_shape=[shape((hidden, block), F32), shape((hidden, block), BF16)],
        in_specs=[vmem] * 2,
        out_specs=[vmem] * 2,
        compiler_params=small,
        cost_estimate=cost,
    )(partial, xor_permute(partial_sent, "chan", channel_axis, 1))
    first = lax.ppermute(pair_sent, "chan", [(c, c ^ (2 if c % 2 else 6)) for c in range(channel_axis)])
    second = lax.ppermute(pair_sent, "chan", [(c, c ^ (4 if c % 2 else 0)) for c in range(channel_axis)])
    half_sum, half_sent = pl.pallas_call(
        sum_kernel,
        out_shape=[shape((hidden, block), F32), shape((hidden, block), BF16)],
        in_specs=[vmem] * 3 + [space],
        out_specs=[vmem] * 2,
        compiler_params=small,
        cost_estimate=cost,
    )(pair, first, second, token)
    other_half = xor_permute(half_sent, "chan", channel_axis, 1)

    grad_in, grad_hidden = pl.pallas_call(
        final_kernel,
        out_shape=[shape((4, rows, block), BF16), shape((hidden, block), F32)],
        in_specs=[vmem] * 6,
        out_specs=[vmem] * 2,
        compiler_params=small,
        cost_estimate=cost,
    )(made_in[0], *got_in, half_sum, other_half)
    return grad_in.reshape(channels, block), grad_filt.reshape(channels, block), grad_hidden


def body_any(blocks, inputs, grad_out, filt, rates, mix_weight):
    channels, block = inputs.shape
    rows = channels // blocks
    total = blocks * block
    half = block // 2
    me = lax.axis_index("seq")
    forward, back = (jnp.asarray(t) for t in tables(block))
    sign = jnp.where(jnp.arange(block) < half, 1.0, -1.0).astype(F32)

    def spread(value):
        return lax.all_to_all(value.reshape(blocks, rows, block), "seq", 0, 0, tiled=True)

    def spectrum(value):
        spec = dot(value, forward)
        return spec[..., :block], spec[..., block:]

    def correlate_blocks(g, z):
        sums = []
        for d in range(blocks):
            gr, gi, zr, zi = g[0][d:], g[1][d:], z[0][: blocks - d], z[1][: blocks - d]
            sums.append(((gr * zr + gi * zi).sum(0), (gi * zr - gr * zi).sum(0)))
        sums.append((jnp.zeros_like(sums[0][0]),) * 2)
        out = [
            jnp.concatenate([sums[d][0] + sign * sums[d + 1][1], sums[d][1] - sign * sums[d + 1][0]], axis=-1)
            for d in range(blocks)
        ]
        return dot(jnp.stack(out).astype(BF16), back)

    spec_g = spectrum(spread(grad_out))
    grad_filt = correlate_blocks(spec_g, spectrum(spread(inputs)))
    grad_in = correlate_blocks(spec_g, spectrum(spread(filt)))
    grad_in = spread(grad_in.astype(BF16)).reshape(channels, block)
    grad_filt = lax.all_to_all(grad_filt, "seq", 0, 0, tiled=True).reshape(channels, block)
    lags = (me * block + jnp.arange(block, dtype=jnp.int32)).astype(F32)
    windowed = grad_filt * jnp.exp(-rates[:, None] * lags[None, :] / total)
    high = windowed.astype(BF16)
    low = (windowed - high.astype(F32)).astype(BF16)
    grad_hidden = lax.psum(dot(mix_weight.T, high) + dot(mix_weight.T, low), "chan")
    return grad_in, grad_filt, grad_hidden


def solution(mesh):
    blocks, chan = mesh.shape["seq"], mesh.shape["chan"]

    def body(inputs, grad_out, filt, rates, mix_weight):
        if blocks == 4 and chan & (chan - 1) == 0 and inputs.shape[0] % 512 == 0 and inputs.shape[1] % 256 == 0:
            return body_four(chan, inputs, grad_out, filt, rates, mix_weight)
        return body_any(blocks, inputs, grad_out, filt, rates, mix_weight)

    return jax.shard_map(
        body,
        mesh=mesh,
        in_specs=(P("chan", "seq"), P("chan", "seq"), P("chan", "seq"), P("chan"), P("chan", None)),
        out_specs=(P("chan", "seq"), P("chan", "seq"), P(None, "seq")),
        check_vma=False,
    )
```

```python
import functools

import jax
import jax.numpy as jnp
import ml_dtypes
import numpy as np
from jax import lax
from jax.experimental import pallas as pl
from jax.experimental.pallas import tpu as pltpu
from jax.sharding import PartitionSpec as P

F32 = jnp.float32
BF16 = jnp.bfloat16


def tables(block):
    k = np.concatenate([np.arange(0, block, 2), np.arange(1, block, 2)]).astype(np.float64)
    phase = np.pi * (k[None, :] + 0.5) * np.arange(block, dtype=np.float64)[:, None] / block
    forward = np.concatenate([np.cos(phase), -np.sin(phase)], axis=1)
    back = forward.T / block
    return forward.astype(ml_dtypes.bfloat16), back.astype(ml_dtypes.bfloat16)


def dot(left, right):
    return jnp.dot(left, right, preferred_element_type=F32)


def xor_permute(value, axis, size, k):
    return lax.ppermute(value, axis, [(j, j ^ k) for j in range(size)])


def correlate(rows, block, spec_g, spec_z, prod):
    half = block // 2
    step = 16

    def chunk(c, carry):
        at = pl.ds(pl.multiple_of(c * step, step), step)
        for part, sign in ((0, 1.0), (1, -1.0)):
            re = pl.ds(part * half, half)
            im = pl.ds(block + part * half, half)
            g = [(spec_g[j, at, re], spec_g[j, at, im]) for j in range(4)]
            z = [(spec_z[j, at, re], spec_z[j, at, im]) for j in range(4)]
            later = None
            for d in (3, 2, 1, 0):
                sum_re = sum_im = None
                for j in range(d, 4):
                    gr, gi = g[j]
                    zr, zi = z[j - d]
                    term_re = gr * zr + gi * zi
                    term_im = gi * zr - gr * zi
                    sum_re = term_re if sum_re is None else sum_re + term_re
                    sum_im = term_im if sum_im is None else sum_im + term_im
                if later is None:
                    out_re, out_im = sum_re, sum_im
                elif sign > 0:
                    out_re, out_im = sum_re + later[1], sum_im - later[0]
                else:
                    out_re, out_im = sum_re - later[1], sum_im + later[0]
                prod[d, at, re] = out_re.astype(BF16)
                prod[d, at, im] = out_im.astype(BF16)
                later = (sum_re, sum_im)
        return carry

    lax.fori_loop(0, rows // step, chunk, 0, unroll=True)


def window_kernel(rows, block, total, rates_ref, f_ref, decay, f_out):
    del f_ref, f_out
    lags = lax.broadcasted_iota(jnp.int32, (rows, block), 1) + lax.axis_index("seq") * block
    for n in range(4):
        rates = jnp.broadcast_to(rates_ref[:, n * rows : (n + 1) * rows], (block, rows)).T
        decay[n] = jnp.exp(-rates * lags.astype(F32) / total)


def filter_kernel(rows, s0, s1, s2, s3, table, back, *refs):
    outs, (spec_g, spec_z, prod) = refs[:4], refs[4:]
    me = lax.axis_index("seq")
    for k, slot in enumerate((s0, s1, s2, s3)):
        spec = dot(slot[...], table[...])
        spec_g[me ^ k] = spec[:rows]
        spec_z[me ^ k] = spec[rows:]
    correlate(rows, table.shape[0], spec_g, spec_z, prod)
    for k, out in enumerate(outs):
        out[...] = dot(prod[me ^ k], back[...]).astype(out.dtype)


def input_kernel(rows, s0, s1, s2, s3, f0, f1, f2, f3, table, back, *refs):
    outs, (spec_g, spec_z, prod) = refs[:4], refs[4:]
    me = lax.axis_index("seq")
    for k, (slot, f) in enumerate(((s0, f0), (s1, f1), (s2, f2), (s3, f3))):
        spec_g[me ^ k] = dot(slot[:rows], table[...])
        spec_z[me ^ k] = dot(f[...], table[...])
    correlate(rows, table.shape[0], spec_g, spec_z, prod)
    for k, out in enumerate(outs):
        out[...] = dot(prod[me ^ k], back[...]).astype(out.dtype)


def hidden_kernel(rows, w0, w1, w2, w3, decay, mix, after, hidden, sent):
    del after
    me = lax.axis_index("seq")
    total = None
    for k, w in enumerate((w0, w1, w2, w3)):
        windowed = w[...].astype(F32) * decay[me ^ k]
        high = windowed.astype(BF16)
        low = (windowed - high.astype(F32)).astype(BF16)
        weight = mix[:, pl.ds(pl.multiple_of((me ^ k) * rows, rows), rows)]
        term = dot(weight, high) + dot(weight, low)
        total = term if total is None else total + term
    hidden[...] = total
    sent[...] = total.astype(BF16)


def unpack_kernel(w0, w1, w2, w3, filt_out, token):
    me = lax.axis_index("seq")
    for k, w in enumerate((w0, w1, w2, w3)):
        filt_out[me ^ k] = w[...].astype(F32)
    token[...] = jnp.zeros_like(token)


def pair_kernel(own, other, out, sent):
    total = own[...] + other[...].astype(F32)
    out[...] = total
    sent[...] = total.astype(BF16)


def sum_kernel(pair, first, second, token, out, sent):
    del token
    lead = lax.axis_index("chan") % 2 == 1
    total = first[...].astype(F32) + jnp.where(lead, second[...].astype(F32), pair[...])
    out[...] = total
    sent[...] = total.astype(BF16)


def final_kernel(v0, v1, v2, v3, own, other, in_out, hidden_out):
    me = lax.axis_index("seq")
    for k, v in enumerate((v0, v1, v2, v3)):
        in_out[me ^ k] = v[...].astype(BF16)
    hidden_out[...] = own[...] + other[...].astype(F32)


def body_four(channel_axis, inputs, grad_out, filt, rates, mix_weight):
    channels, block = inputs.shape
    rows = channels // 4
    total = 4 * block
    hidden = mix_weight.shape[1]
    forward, back = (jnp.asarray(t) for t in tables(block))
    shape = jax.ShapeDtypeStruct
    vmem = pl.BlockSpec(memory_space=pltpu.VMEM)
    params = pltpu.CompilerParams(vmem_limit_bytes=8 * 1024 * 1024)
    small = pltpu.CompilerParams(vmem_limit_bytes=4 * 1024 * 1024)
    cost = pl.CostEstimate(flops=1000, bytes_accessed=1000, transcendentals=0)
    scratch = [
        pltpu.VMEM((4, rows, 2 * block), F32),
        pltpu.VMEM((4, rows, 2 * block), F32),
        pltpu.VMEM((4, rows, 2 * block), BF16),
    ]

    me = lax.axis_index("seq")
    arrays = jnp.stack([value.reshape(4, rows, block) for value in (grad_out, inputs)], 1)
    slots = [lax.dynamic_index_in_dim(arrays, me ^ k, 0, keepdims=False).reshape(2 * rows, block) for k in range(4)]
    slots_f = [lax.dynamic_index_in_dim(filt.reshape(4, rows, block), me ^ k, 0, keepdims=False) for k in range(4)]
    space = pl.BlockSpec(memory_space=pl.ANY)
    decay, slots_f[1] = pl.pallas_call(
        functools.partial(window_kernel, rows, block, total),
        out_shape=[shape((4, rows, block), F32), shape((rows, block), BF16)],
        in_specs=[vmem, space],
        out_specs=[vmem, space],
        input_output_aliases={1: 1},
        compiler_params=pltpu.CompilerParams(vmem_limit_bytes=60 * 1024 * 1024),
        cost_estimate=cost,
    )(rates.reshape(1, channels), slots_f[1])
    slots = slots[:1] + [xor_permute(slots[k], "seq", 4, k) for k in (1, 2, 3)]
    slots_f = slots_f[:1] + [xor_permute(slots_f[k], "seq", 4, k) for k in (1, 2, 3)]

    made = pl.pallas_call(
        functools.partial(filter_kernel, rows),
        out_shape=[shape((rows, block), F32)] + [shape((rows, block), BF16)] * 3,
        in_specs=[vmem] * 6,
        out_specs=[vmem] * 4,
        scratch_shapes=scratch,
        compiler_params=params,
        cost_estimate=cost,
    )(*slots, forward, back)
    got = [xor_permute(made[k], "seq", 4, k) for k in (1, 2, 3)]

    made_in = pl.pallas_call(
        functools.partial(input_kernel, rows),
        out_shape=[shape((rows, block), BF16)] + [shape((rows, block), F32)] * 3,
        in_specs=[vmem] * 10,
        out_specs=[vmem] * 4,
        scratch_shapes=scratch,
        compiler_params=params,
        cost_estimate=cost,
    )(*slots, *slots_f, forward, back)
    got_in = [xor_permute(made_in[k], "seq", 4, k) for k in (1, 2, 3)]

    partial, partial_sent = pl.pallas_call(
        functools.partial(hidden_kernel, rows),
        out_shape=[shape((hidden, block), F32), shape((hidden, block), BF16)],
        in_specs=[vmem] * 6 + [space],
        out_specs=[vmem] * 2,
        compiler_params=small,
        cost_estimate=cost,
    )(made[0], *got, decay, mix_weight.T, made_in[1])
    grad_filt, token = pl.pallas_call(
        unpack_kernel,
        out_shape=[shape((4, rows, block), F32), shape((8, 128), F32)],
        in_specs=[vmem] * 4,
        out_specs=[vmem] * 2,
        compiler_params=small,
        cost_estimate=cost,
    )(made[0], *got)
    pair, pair_sent = pl.pallas_call(
        pair_kernel,
        out_shape=[shape((hidden, block), F32), shape((hidden, block), BF16)],
        in_specs=[vmem] * 2,
        out_specs=[vmem] * 2,
        compiler_params=small,
        cost_estimate=cost,
    )(partial, xor_permute(partial_sent, "chan", channel_axis, 1))
    first = lax.ppermute(pair_sent, "chan", [(c, c ^ (2 if c % 2 else 6)) for c in range(channel_axis)])
    second = lax.ppermute(pair_sent, "chan", [(c, c ^ (4 if c % 2 else 0)) for c in range(channel_axis)])
    half_sum, half_sent = pl.pallas_call(
        sum_kernel,
        out_shape=[shape((hidden, block), F32), shape((hidden, block), BF16)],
        in_specs=[vmem] * 3 + [space],
        out_specs=[vmem] * 2,
        compiler_params=small,
        cost_estimate=cost,
    )(pair, first, second, token)
    other_half = xor_permute(half_sent, "chan", channel_axis, 1)

    grad_in, grad_hidden = pl.pallas_call(
        final_kernel,
        out_shape=[shape((4, rows, block), BF16), shape((hidden, block), F32)],
        in_specs=[vmem] * 6,
        out_specs=[vmem] * 2,
        compiler_params=small,
        cost_estimate=cost,
    )(made_in[0], *got_in, half_sum, other_half)
    return grad_in.reshape(channels, block), grad_filt.reshape(channels, block), grad_hidden


def body_any(blocks, inputs, grad_out, filt, rates, mix_weight):
    channels, block = inputs.shape
    rows = channels // blocks
    total = blocks * block
    half = block // 2
    me = lax.axis_index("seq")
    forward, back = (jnp.asarray(t) for t in tables(block))
    sign = jnp.where(jnp.arange(block) < half, 1.0, -1.0).astype(F32)

    def spread(value):
        return lax.all_to_all(value.reshape(blocks, rows, block), "seq", 0, 0, tiled=True)

    def spectrum(value):
        spec = dot(value, forward)
        return spec[..., :block], spec[..., block:]

    def correlate_blocks(g, z):
        sums = []
        for d in range(blocks):
            gr, gi, zr, zi = g[0][d:], g[1][d:], z[0][: blocks - d], z[1][: blocks - d]
            sums.append(((gr * zr + gi * zi).sum(0), (gi * zr - gr * zi).sum(0)))
        sums.append((jnp.zeros_like(sums[0][0]),) * 2)
        out = [
            jnp.concatenate([sums[d][0] + sign * sums[d + 1][1], sums[d][1] - sign * sums[d + 1][0]], axis=-1)
            for d in range(blocks)
        ]
        return dot(jnp.stack(out).astype(BF16), back)

    spec_g = spectrum(spread(grad_out))
    grad_filt = correlate_blocks(spec_g, spectrum(spread(inputs)))
    grad_in = correlate_blocks(spec_g, spectrum(spread(filt)))
    grad_in = spread(grad_in.astype(BF16)).reshape(channels, block)
    grad_filt = lax.all_to_all(grad_filt, "seq", 0, 0, tiled=True).reshape(channels, block)
    lags = (me * block + jnp.arange(block, dtype=jnp.int32)).astype(F32)
    windowed = grad_filt * jnp.exp(-rates[:, None] * lags[None, :] / total)
    high = windowed.astype(BF16)
    low = (windowed - high.astype(F32)).astype(BF16)
    grad_hidden = lax.psum(dot(mix_weight.T, high) + dot(mix_weight.T, low), "chan")
    return grad_in, grad_filt, grad_hidden


def solution(mesh):
    blocks, chan = mesh.shape["seq"], mesh.shape["chan"]

    def body(inputs, grad_out, filt, rates, mix_weight):
        if blocks == 4 and chan & (chan - 1) == 0 and inputs.shape[0] % 512 == 0 and inputs.shape[1] % 256 == 0:
            return body_four(chan, inputs, grad_out, filt, rates, mix_weight)
        return body_any(blocks, inputs, grad_out, filt, rates, mix_weight)

    return jax.shard_map(
        body,
        mesh=mesh,
        in_specs=(P("chan", "seq"), P("chan", "seq"), P("chan", "seq"), P("chan"), P("chan", None)),
        out_specs=(P("chan", "seq"), P("chan", "seq"), P(None, "seq")),
        check_vma=False,
    )
```
